512 devices in a mesh: rows: 32 (over x, y), heads: 16 (over z, core).
Axes of the slice: x: 4, y: 8, z: 8, core: 2. Of those that a mesh axis runs over, the one named last changes fastest.
Arguments:
- queries: bfloat16 [8, 256, 4096], P(None, 'rows', 'heads'), may hold values from -6 to 6
- keys: bfloat16 [8, 256, 4096], P(None, 'rows', 'heads'), may hold values from -0.375 to 0.375
- values: bfloat16 [8, 256, 8192], P(None, 'rows', 'heads'), may hold values from -6 to 6
- gates: bfloat16 [8, 256, 8192], P(None, 'rows', 'heads'), may hold values from -6 to 6
- prefill_states: bfloat16 [256, 16, 256, 512], P('rows', 'heads'), may hold values from -0.375 to 0.375
- dest_slot: int32 [256], P('rows'), may hold values from 0 to 255, as said below
- arrive_step: int32 [256], P('rows'), may hold values from 0 to 7
- decay: float32 [16], P('heads'), may hold values from 0.3 to 0.98
- norm_gain: float32 [8192], P('heads'), may hold values from 0.1 to 1.9
- out_weight: bfloat16 [8192, 2048], P('heads'), may hold values from -0.0625 to 0.0625
Outputs:
- mixed: bfloat16 [8, 256, 2048], P(None, 'rows', 'heads')
The draws below stay inside these ranges and needn't reach their ends.
Inputs may be any that keep to these rules, and one draw needn't show every extreme that they name: `dest_slot`: every slot is named exactly once. Request s * 8 + j (j < 8) joins a slot on index (s + j * 4) mod 32 of rows.
All inputs are finite; a program needn't handle non-finite values.
Results may differ from the reference program's by a relative error of at most 0.0049.
Values may be sent and summed in bfloat16 or wider, within the bound.
No kernel may reach another device: no remote copies, remote signals or barrier semaphores. Data moves between devices by JAX's collectives and lax.ppermute only.
A program may use at most 64 MiB of HBM per device.

```python
import math
import jax
import jax.numpy as jnp
from jax import lax

DK = 256
DV = 512
DW = 2048
R_DEV = 8
ARR_DEV = 8
STEPS = 8
HEADS = 16
ROWS = 256
ARRIVALS = 256


def draw_dest_slot(key, part):
    key = jax.random.fold_in(key, 11)
    peers = ARRIVALS // ARR_DEV
    spacing = peers // ARR_DEV
    request = jnp.arange(ARRIVALS, dtype=jnp.int32)
    source = request // ARR_DEV
    second = request % ARR_DEV
    device = (source + second * spacing) % peers
    slot_keys = jax.random.split(key, peers)
    slot_order = jax.vmap(lambda single: jax.random.permutation(single, R_DEV))(slot_keys)
    return (device * R_DEV + slot_order[device, second]).astype(jnp.int32)


def set_ends(drawn, key, smallest, largest):
    dims = drawn.shape
    place = [jax.random.randint(jax.random.fold_in(key, axis), (), 0, dims[axis]) for axis in range(len(dims))]
    drawn = drawn.at[tuple(place)].set(smallest)
    longest = dims.index(max(dims))
    place[longest] = (place[longest] + 1) % dims[longest]
    return drawn.at[tuple(place)].set(largest)


def shard_levels(key, shape, cuts, low, largest):
    loudness = 1.0
    for position, blocks in cuts:
        heights = jax.random.uniform(jax.random.fold_in(jax.random.fold_in(key, 6), position), (blocks,), jnp.float32, low / len(cuts), largest / len(cuts))
        loudness = loudness * jnp.repeat(jnp.exp(heights), shape[position] // blocks).reshape((-1,) + (1,) * (len(shape) - 1 - position))
    return loudness


def scatter_about(own_key, shape, deviation, most, pieces=(), kind=jnp.bfloat16):
    drawn = deviation * jax.random.normal(own_key, shape, jnp.float32)
    if pieces:
        drawn = drawn * shard_levels(own_key, shape, pieces, -0.22, 0.18)
    return jnp.clip(drawn, -most, most).astype(kind)


def setup_inputs(seed: int = 0) -> dict:
    key_list = jax.random.split(jax.random.key(seed), 11)
    return {
        "queries": scatter_about(key_list[0], (STEPS, ROWS, HEADS * DK), 1.0, 6.0, ((1, 32), (2, 16))),
        "keys": scatter_about(key_list[1], (STEPS, ROWS, HEADS * DK), 0.0625, 0.375, ((1, 32), (2, 16))),
        "values": scatter_about(key_list[2], (STEPS, ROWS, HEADS * DV), 1.0, 6.0, ((1, 32), (2, 16))),
        "gates": scatter_about(key_list[3], (STEPS, ROWS, HEADS * DV), 1.0, 6.0, ((1, 32), (2, 16))),
        "prefill_states": scatter_about(key_list[4], (ARRIVALS, HEADS, DK, DV), 0.0625, 0.375, ((0, 32), (1, 16))),
        "dest_slot": draw_dest_slot(jax.random.fold_in(key_list[10], 71), 0),
        "arrive_step": set_ends(jax.random.randint(key_list[6], (ARRIVALS,), 0, STEPS), jax.random.fold_in(key_list[6], 1), 0, STEPS - 1).astype(jnp.int32),
        "decay": jnp.clip(jnp.exp(math.log(0.98) - 1.1837701 * jax.random.uniform(key_list[7], (HEADS,), jnp.float32) ** shard_levels(key_list[7], (HEADS,), ((0, 16),), -0.2, 0.2)), 0.3, 0.98),
        "norm_gain": jnp.clip(1.0 + 0.18 * jax.random.normal(key_list[8], (HEADS * DV,), jnp.float32), 0.1, 1.9),
        "out_weight": scatter_about(key_list[9], (HEADS * DV, DW), (HEADS * DV) ** -0.5, 0.0625, ((0, 16),)),
    }


def reference(queries, keys, values, gates, prefill_states, dest_slot, arrive_step, decay, norm_gain, out_weight):
    step_count = queries.shape[0]
    row_count = queries.shape[1]
    head_count = prefill_states.shape[1]
    slot_ids = jnp.arange(row_count, dtype=jnp.int32)
    matches = dest_slot[None, :] == slot_ids[:, None]
    join_step = lax.optimization_barrier(jnp.sum(jnp.where(matches, arrive_step[None, :] + 1, 0), axis=1)) - 1
    select = matches.astype(jnp.float32)
    q_all = queries.reshape(step_count, row_count, head_count, DK)
    k_all = keys.reshape(step_count, row_count, head_count, DK)
    v_all = values.reshape(step_count, row_count, head_count, DV)
    g_all = gates.reshape(step_count, row_count, head_count, DV)

    def one_head(head):
        source = lax.dynamic_index_in_dim(prefill_states, head, 1, keepdims=False).astype(jnp.float32)
        incoming = jnp.einsum('ra,akv->rkv', select, source, precision=lax.Precision.HIGHEST)
        decay_rate = decay[head]
        gains = lax.dynamic_slice_in_dim(norm_gain, head * DV, DV)
        q_head = lax.dynamic_index_in_dim(q_all, head, 2, keepdims=False).astype(jnp.float32)
        k_head = lax.dynamic_index_in_dim(k_all, head, 2, keepdims=False).astype(jnp.float32)
        v_head = lax.dynamic_index_in_dim(v_all, head, 2, keepdims=False).astype(jnp.float32)
        g_head = lax.dynamic_index_in_dim(g_all, head, 2, keepdims=False).astype(jnp.float32)
        carried = jnp.zeros((row_count, DK, DV), jnp.float32)
        results = []
        for step_now in range(step_count):
            carried = jnp.where((join_step == step_now)[:, None, None], incoming, carried)
            carried = decay_rate * carried + k_head[step_now][:, :, None] * v_head[step_now][:, None, :]
            readout = jnp.einsum('rk,rkv->rv', q_head[step_now], carried, precision=lax.Precision.HIGHEST)
            inv_rms = lax.rsqrt(lax.optimization_barrier(jnp.mean(readout * readout, axis=-1, keepdims=True)) + 1e-06)
            results.append((readout * inv_rms * gains * g_head[step_now]).astype(jnp.bfloat16))
        return jnp.stack(results)
    normed = lax.map(one_head, jnp.arange(head_count, dtype=jnp.int32))
    flattened = jnp.transpose(normed, (1, 2, 0, 3)).reshape(step_count * row_count, head_count * DV)
    projected = jnp.dot(flattened, out_weight, preferred_element_type=jnp.float32)
    return projected.astype(jnp.bfloat16).reshape(step_count, row_count, out_weight.shape[1])
```

```python
import jax
import jax.numpy as jnp
from jax import lax
from jax.experimental import pallas as pl
from jax.experimental.pallas import tpu as pltpu
from jax.sharding import PartitionSpec as P

F32 = jnp.float32
BF16 = jnp.bfloat16
VMEM = pl.BlockSpec(memory_space=pltpu.VMEM)
SMEM = pl.BlockSpec(memory_space=pltpu.SMEM)
PAD = 16


def int_power(base, exponent, most):
    result = jnp.ones_like(exponent, dtype=F32)
    for below in range(most):
        result = jnp.where(exponent > below, result * base, result)
    return result


def source_kernel(steps, slots, member_ref, dest_ref, step_ref, decay_ref, q_ref, state_ref, out_ref):
    peers = q_ref.shape[0]
    width = state_ref.shape[2]
    member = member_ref[0]
    decay = decay_ref[0]
    row = lax.broadcasted_iota(jnp.int32, (steps * slots, 128), 0)
    line = lax.broadcasted_iota(jnp.int32, (PAD, 128), 0)
    for peer in range(peers):
        order = lax.rem(peer - member + peers, peers)
        slot = lax.rem(dest_ref[order], slots)
        joined = step_ref[order]
        full = jnp.dot(q_ref[peer], state_ref[order], preferred_element_type=F32)
        age = lax.div(row, slots) - joined + 1
        factor = jnp.where((lax.rem(row, slots) == slot) & (age > 0), int_power(decay, age, steps), 0.0)
        for col in range(0, width, 128):
            part = full[:, col : col + 128] * factor
            part = jnp.sum(part.reshape(steps, slots, 128), axis=1)
            tail = jnp.where(line[:PAD - steps] == 0, slot if col == 0 else joined, 0).astype(F32)
            out_ref[peer, :, col : col + 128] = jnp.concatenate([part, tail], axis=0).astype(BF16)


def row_kernel(steps, slots, decay_ref, back_ref, q_ref, k_ref, v_ref, g_ref, gain_ref, w_ref, out_ref):
    rows = steps * slots
    width = v_ref.shape[1]
    decay = decay_ref[0]
    back = back_ref[...]
    lines = back.shape[0]
    head = back[:, 0:256].astype(F32)
    here = lax.broadcasted_iota(jnp.int32, (lines, lines), 0)
    there = lax.broadcasted_iota(jnp.int32, (lines, lines), 1)
    pick = here == lax.div(there, PAD) * PAD + steps
    slot_of = jnp.sum(jnp.where(pick, head[:, 0:lines], 0.0), axis=0, keepdims=True).astype(jnp.int32)
    step_of = jnp.sum(jnp.where(pick, head[:, 128 : 128 + lines], 0.0), axis=0, keepdims=True)
    row = lax.broadcasted_iota(jnp.int32, (rows, lines), 0)
    line = lax.broadcasted_iota(jnp.int32, (rows, lines), 1)
    one = (lax.rem(row, slots) == slot_of) & (lax.div(row, slots) == lax.rem(line, PAD))
    join = jnp.sum(jnp.where(one, step_of, 0.0), axis=1, keepdims=True).astype(jnp.int32)
    later = lax.broadcasted_iota(jnp.int32, (rows, rows), 0)
    earlier = lax.broadcasted_iota(jnp.int32, (rows, rows), 1)
    t_now, t_then = lax.div(later, slots), lax.div(earlier, slots)
    kept = (lax.rem(later, slots) == lax.rem(earlier, slots)) & (t_then <= t_now)
    kept = kept & ((t_then >= join) | (t_now < join))
    scores = lax.dot_general(q_ref[...], k_ref[...], (((1,), (1,)), ((), ())), preferred_element_type=F32)
    weights = jnp.where(kept, scores * int_power(decay, t_now - t_then, steps - 1), 0.0)
    coarse = weights.astype(BF16)
    fine = (weights - coarse.astype(F32)).astype(BF16)
    v = v_ref[...]
    readout = jnp.dot(jnp.where(one, 1.0, 0.0).astype(BF16), back, preferred_element_type=F32)
    readout += jnp.dot(coarse, v, preferred_element_type=F32)
    readout += jnp.dot(fine, v, preferred_element_type=F32)
    mean = jnp.sum(readout * readout, axis=1, keepdims=True) * (1.0 / width)
    normed = readout * lax.rsqrt(mean + 1e-06) * gain_ref[...] * g_ref[...].astype(F32)
    normed = normed.astype(BF16)
    shares, _, columns = out_ref.shape
    for share in range(shares):
        part = jnp.dot(normed, w_ref[:, share * columns : (share + 1) * columns], preferred_element_type=F32)
        out_ref[share] = part.astype(out_ref.dtype)


def shards(queries, keys, values, gates, prefill_states, dest_slot, arrive_step, decay, norm_gain, out_weight):
    steps, slots, key_dim = queries.shape
    val_dim = values.shape[2]
    rows = steps * slots
    per_source = dest_slot.shape[0]
    peers = lax.axis_size("rows")
    spacing = peers // per_source
    groups = [[first + spacing * m for m in range(per_source)] for first in range(spacing)]
    member = (lax.axis_index("rows") // spacing).astype(jnp.int32).reshape(1)
    q = queries.reshape(rows, key_dim)
    q_all = lax.all_to_all(
        jnp.broadcast_to(q[None], (per_source, rows, key_dim)),
        "rows", 0, 0, axis_index_groups=groups, tiled=True,
    )
    lines = per_source * PAD
    readouts = pl.pallas_call(
        lambda *refs: source_kernel(steps, slots, *refs),
        out_shape=jax.ShapeDtypeStruct((per_source, PAD, val_dim), BF16),
        in_specs=[SMEM] * 4 + [VMEM] * 2,
        out_specs=VMEM,
        compiler_params=pltpu.CompilerParams(vmem_limit_bytes=16 << 20),
        name="source_readout",
    )(member, dest_slot, arrive_step, decay, q_all, prefill_states.reshape(per_source, key_dim, val_dim))
    back = lax.all_to_all(readouts, "rows", 0, 0, axis_index_groups=groups, tiled=True)
    heads = lax.axis_size("heads")
    columns = out_weight.shape[1] // heads
    partial = pl.pallas_call(
        lambda *refs: row_kernel(steps, slots, *refs),
        out_shape=jax.ShapeDtypeStruct((heads, rows, columns), BF16),
        in_specs=[SMEM] + [VMEM] * 7,
        out_specs=VMEM,
        compiler_params=pltpu.CompilerParams(vmem_limit_bytes=16 << 20),
        name="combine_project",
    )(
        decay, back.reshape(lines, val_dim), q, keys.reshape(rows, key_dim), values.reshape(rows, val_dim),
        gates.reshape(rows, val_dim), norm_gain.reshape(1, val_dim), out_weight,
    )
    shares = lax.all_to_all(partial, "heads", 0, 0, tiled=True)
    total = jnp.sum(shares.astype(F32), axis=0)
    return total.astype(BF16).reshape(steps, slots, columns)


def solution(mesh):
    placed = (
        P(None, "rows", "heads"),
        P(None, "rows", "heads"),
        P(None, "rows", "heads"),
        P(None, "rows", "heads"),
        P("rows", "heads", None, None),
        P("rows"),
        P("rows"),
        P("heads"),
        P("heads"),
        P("heads", None),
    )
    return jax.shard_map(
        shards, mesh=mesh, in_specs=placed, out_specs=P(None, "rows", "heads"), check_vma=False
    )
```

```python
import jax
import jax.numpy as jnp
from jax import lax
from jax.experimental import pallas as pl
from jax.experimental.pallas import tpu as pltpu
from jax.sharding import PartitionSpec as P

F32 = jnp.float32
BF16 = jnp.bfloat16
VMEM = pl.BlockSpec(memory_space=pltpu.VMEM)
SMEM = pl.BlockSpec(memory_space=pltpu.SMEM)
ANY = pl.BlockSpec(memory_space=pl.ANY)
TAIL = 128


def in_hbm(value):
    return pltpu.with_memory_space_constraint(value, pltpu.HBM)


def int_power(base, exponent, most):
    result = jnp.ones_like(exponent, dtype=F32)
    for below in range(most):
        result = jnp.where(exponent > below, result * base, result)
    return result


def prepare_kernel(
    spacing, steps, slots, dest_in, step_in, decay_ref, q_in, state_in,
    spread_ref, state_ref, factor_ref, tail_ref, q_ref, dest_ref, step_ref, sems,
):
    peers = factor_ref.shape[0]
    first = pltpu.make_async_copy(q_in, q_ref, sems.at[0])
    ints = [
        pltpu.make_async_copy(dest_in, dest_ref, sems.at[1]),
        pltpu.make_async_copy(step_in, step_ref, sems.at[2]),
    ]
    copies = [first] + ints + [
        pltpu.make_async_copy(state_in.at[order], state_ref.at[order], sems.at[3 + order]) for order in range(peers)
    ]
    for copy in copies:
        copy.start()
    first.wait()
    for peer in range(peers):
        spread_ref[peer] = q_ref[...]
    for copy in ints:
        copy.wait()
    member = lax.div(lax.axis_index("rows"), spacing)
    decay = decay_ref[0]
    row = lax.broadcasted_iota(jnp.int32, (steps * slots, 128), 0)
    lane = lax.broadcasted_iota(jnp.int32, (steps, TAIL), 1)
    for order in range(peers):
        slot = lax.rem(dest_ref[order], slots)
        joined = step_ref[order]
        age = lax.div(row, slots) - joined + 1
        mine = (lax.rem(row, slots) == slot) & (age > 0)
        peer = lax.rem(member + order, peers)
        factor_ref[peer] = jnp.where(mine, int_power(decay, age, steps), 0.0)
        tail_ref[peer] = jnp.where(lane < TAIL // 2, slot, joined).astype(F32)
    for copy in copies[3:]:
        copy.wait()


def source_kernel(spacing, steps, slots, q_ref, state_ref, factor_ref, tail_ref, out_ref):
    peers, _, width = state_ref.shape
    member = lax.div(lax.axis_index("rows"), spacing)
    for peer in range(peers):
        order = lax.rem(peer - member + peers, peers)
        full = jnp.dot(q_ref[peer], state_ref[order], preferred_element_type=F32)
        factor = factor_ref[peer]
        parts = []
        for col in range(0, width, 128):
            part = full[:, col : col + 128] * factor
            parts.append(jnp.sum(part.reshape(steps, slots, 128), axis=1))
        parts.append(tail_ref[peer])
        out_ref[peer] = jnp.concatenate(parts, axis=1).astype(BF16)


def row_kernel(steps, slots, decay_ref, back_ref, q_ref, k_ref, v_ref, g_ref, gain_ref, w_ref, out_ref):
    rows = steps * slots
    width = v_ref.shape[1]
    decay = decay_ref[0]
    back = back_ref[...].astype(F32)
    lines = back.shape[0] * back.shape[1]
    back = back.reshape(lines, back.shape[2])
    here = lax.broadcasted_iota(jnp.int32, (lines, TAIL), 0)
    there = lax.broadcasted_iota(jnp.int32, (lines, TAIL), 1)
    pick = here == lax.rem(there, TAIL // 2)
    facts = jnp.sum(jnp.where(pick, back[:, width:], 0.0), axis=0, keepdims=True)
    slot_of = facts[:, 0:lines].astype(jnp.int32)
    step_of = facts[:, TAIL // 2 : TAIL // 2 + lines]
    row = lax.broadcasted_iota(jnp.int32, (rows, lines), 0)
    line = lax.broadcasted_iota(jnp.int32, (rows, lines), 1)
    one = (lax.rem(row, slots) == slot_of) & (lax.div(row, slots) == lax.rem(line, steps))
    join = jnp.sum(jnp.where(one, step_of, 0.0), axis=1, keepdims=True).astype(jnp.int32)
    later = lax.broadcasted_iota(jnp.int32, (rows, rows), 0)
    earlier = lax.broadcasted_iota(jnp.int32, (rows, rows), 1)
    t_now, t_then = lax.div(later, slots), lax.div(earlier, slots)
    kept = (lax.rem(later, slots) == lax.rem(earlier, slots)) & (t_then <= t_now)
    kept = kept & ((t_then >= join) | (t_now < join))
    scores = lax.dot_general(q_ref[...], k_ref[...], (((1,), (1,)), ((), ())), preferred_element_type=F32)
    weights = jnp.where(kept, scores * int_power(decay, t_now - t_then, steps - 1), 0.0)
    coarse = weights.astype(BF16)
    fine = (weights - coarse.astype(F32)).astype(BF16)
    v = v_ref[...]
    carried = back[:, :width].astype(BF16)
    readout = jnp.dot(jnp.where(one, 1.0, 0.0).astype(BF16), carried, preferred_element_type=F32)
    readout += jnp.dot(coarse, v, preferred_element_type=F32)
    readout += jnp.dot(fine, v, preferred_element_type=F32)
    mean = jnp.sum(readout * readout, axis=1, keepdims=True) * (1.0 / width)
    normed = readout * lax.rsqrt(mean + 1e-06) * gain_ref[...] * g_ref[...].astype(F32)
    normed = normed.astype(BF16)
    shares, _, columns = out_ref.shape
    for share in range(shares):
        part = jnp.dot(normed, w_ref[:, share * columns : (share + 1) * columns], preferred_element_type=F32)
        out_ref[share] = part.astype(out_ref.dtype)


def total_kernel(shares_ref, out_ref):
    total = shares_ref[0].astype(F32)
    for share in range(1, shares_ref.shape[0]):
        total += shares_ref[share].astype(F32)
    out_ref[...] = total.astype(out_ref.dtype)


def call(kernel, name, out_shape, in_specs, out_specs, scratch=(), cost=None):
    return pl.pallas_call(
        kernel,
        out_shape=out_shape,
        in_specs=in_specs,
        out_specs=out_specs,
        scratch_shapes=scratch,
        compiler_params=pltpu.CompilerParams(vmem_limit_bytes=16 << 20),
        cost_estimate=cost,
        name=name,
    )


def shards(queries, keys, values, gates, prefill_states, dest_slot, arrive_step, decay, norm_gain, out_weight):
    steps, slots, key_dim = queries.shape
    val_dim = values.shape[2]
    rows = steps * slots
    per_source = dest_slot.shape[0]
    spacing = lax.axis_size("rows") // per_source
    groups = [[first + spacing * m for m in range(per_source)] for first in range(spacing)]
    shape = jax.ShapeDtypeStruct
    q = queries.reshape(rows, key_dim)
    states = prefill_states.reshape(per_source, key_dim, val_dim)
    spread, held, factor, tail = call(
        lambda *refs: prepare_kernel(spacing, steps, slots, *refs),
        "spread_queries",
        (
            pltpu.VMEM((per_source, rows, key_dim), BF16),
            pltpu.VMEM(states.shape, BF16),
            pltpu.VMEM((per_source, rows, 128), F32),
            pltpu.VMEM((per_source, steps, TAIL), F32),
        ),
        [ANY, ANY, SMEM, ANY, ANY],
        (VMEM,) * 4,
        [
            pltpu.VMEM(q.shape, BF16),
            pltpu.SMEM(dest_slot.shape, jnp.int32),
            pltpu.SMEM(arrive_step.shape, jnp.int32),
            pltpu.SemaphoreType.DMA((3 + per_source,)),
        ],
    )(in_hbm(dest_slot), in_hbm(arrive_step), decay, in_hbm(q), in_hbm(states))
    q_all = lax.all_to_all(spread, "rows", 0, 0, axis_index_groups=groups, tiled=True)
    readouts = call(
        lambda *refs: source_kernel(spacing, steps, slots, *refs),
        "source_readout",
        shape((per_source, steps, val_dim + TAIL), BF16),
        [VMEM] * 4,
        VMEM,
        cost=pl.CostEstimate(flops=2 * rows * states.size, bytes_accessed=32 << 20, transcendentals=0),
    )(q_all, held, factor, tail)
    back = lax.all_to_all(readouts, "rows", 0, 0, axis_index_groups=groups, tiled=True)
    heads = lax.axis_size("heads")
    columns = out_weight.shape[1] // heads
    partial = call(
        lambda *refs: row_kernel(steps, slots, *refs),
        "combine_project",
        shape((heads, rows, columns), BF16),
        [SMEM] + [VMEM] * 7,
        VMEM,
    )(
        decay, back, q, keys.reshape(rows, key_dim), values.reshape(rows, val_dim),
        gates.reshape(rows, val_dim), norm_gain.reshape(1, val_dim), out_weight,
    )
    shares = lax.all_to_all(partial, "heads", 0, 0, tiled=True)
    total = call(total_kernel, "sum_heads", shape((rows, columns), BF16), [VMEM], VMEM)(shares)
    return total.reshape(steps, slots, columns)


def solution(mesh):
    placed = (
        P(None, "rows", "heads"),
        P(None, "rows", "heads"),
        P(None, "rows", "heads"),
        P(None, "rows", "heads"),
        P("rows", "heads", None, None),
        P("rows"),
        P("rows"),
        P("heads"),
        P("heads"),
        P("heads", None),
    )
    return jax.shard_map(
        shards, mesh=mesh, in_specs=placed, out_specs=P(None, "rows", "heads"), check_vma=False
    )
```

```python
import jax
import jax.numpy as jnp
from jax import lax
from jax.experimental import pallas as pl
from jax.experimental.pallas import tpu as pltpu
from jax.sharding import PartitionSpec as P

F32 = jnp.float32
BF16 = jnp.bfloat16
VMEM = pl.BlockSpec(memory_space=pltpu.VMEM)
SMEM = pl.BlockSpec(memory_space=pltpu.SMEM)
ANY = pl.BlockSpec(memory_space=pl.ANY)
TAIL = 128
SOURCE_ORDER = (5, 7, 1, 3, 4, 6, 0, 2)
RETURN_ORDER = (5, 6, 7, 0, 1, 2, 3, 4)
HEAD_ORDER = tuple(range(15, -1, -1))


def in_hbm(value):
    return pltpu.with_memory_space_constraint(value, pltpu.HBM)


def int_power(base, exponent, most):
    result = jnp.ones_like(exponent, dtype=F32)
    for below in range(most):
        result = jnp.where(exponent > below, result * base, result)
    return result


def prepare_kernel(
    spacing, steps, slots, dest_in, step_in, decay_ref, q_in, state_in,
    spread_ref, state_ref, scale_ref, pick_ref, tail_ref, q_ref, dest_ref, step_ref, sems,
):
    peers = scale_ref.shape[0]
    first = pltpu.make_async_copy(q_in, q_ref, sems.at[0])
    ints = [
        pltpu.make_async_copy(dest_in, dest_ref, sems.at[1]),
        pltpu.make_async_copy(step_in, step_ref, sems.at[2]),
    ]
    copies = [first] + ints + [
        pltpu.make_async_copy(state_in.at[order], state_ref.at[order], sems.at[3 + order]) for order in range(peers)
    ]
    for copy in copies:
        copy.start()
    first.wait()
    for peer in range(peers):
        spread_ref[peer] = q_ref[...]
    for copy in ints:
        copy.wait()
    member = lax.div(lax.axis_index("rows"), spacing)
    decay = decay_ref[0]
    line = lax.broadcasted_iota(jnp.int32, (steps, 128), 0)
    place = lax.broadcasted_iota(jnp.int32, (slots, 128), 0)
    lane = lax.broadcasted_iota(jnp.int32, (steps, TAIL), 1)
    for order in range(peers):
        slot = lax.rem(dest_ref[order], slots)
        joined = step_ref[order]
        age = line - joined + 1
        peer = lax.rem(member + order, peers)
        scale_ref[peer] = jnp.where(age > 0, int_power(decay, age, steps), 0.0)
        pick_ref[peer] = jnp.where(place == slot, 1.0, 0.0)
        tail_ref[peer] = jnp.where(lane < TAIL // 2, slot, joined).astype(F32)
    for copy in copies[3:]:
        copy.wait()


def source_kernel(spacing, steps, slots, q_ref, state_ref, scale_ref, pick_ref, tail_ref, out_ref):
    peers, _, width = state_ref.shape
    member = lax.div(lax.axis_index("rows"), spacing)
    for block, peer in enumerate(SOURCE_ORDER):
        order = lax.rem(peer - member + peers, peers)
        full = jnp.dot(q_ref[block], state_ref[order], preferred_element_type=F32)
        scale, pick = scale_ref[peer], pick_ref[peer][None]
        parts = []
        for col in range(0, width, 128):
            part = full[:, col : col + 128].reshape(steps, slots, 128) * pick
            parts.append(jnp.sum(part, axis=1) * scale)
        parts.append(tail_ref[peer])
        out_ref[RETURN_ORDER.index(peer)] = jnp.concatenate(parts, axis=1).astype(BF16)


def row_kernel(steps, slots, decay_ref, back_ref, q_ref, k_ref, v_ref, g_ref, gain_ref, w_ref, out_ref):
    rows = steps * slots
    width = v_ref.shape[1]
    decay = decay_ref[0]
    back = back_ref[...].astype(F32)
    lines = back.shape[0] * back.shape[1]
    back = back.reshape(lines, back.shape[2])
    here = lax.broadcasted_iota(jnp.int32, (lines, TAIL), 0)
    there = lax.broadcasted_iota(jnp.int32, (lines, TAIL), 1)
    pick = here == lax.rem(there, TAIL // 2)
    facts = jnp.sum(jnp.where(pick, back[:, width:], 0.0), axis=0, keepdims=True)
    slot_of = facts[:, 0:lines].astype(jnp.int32)
    step_of = facts[:, TAIL // 2 : TAIL // 2 + lines]
    row = lax.broadcasted_iota(jnp.int32, (rows, lines), 0)
    line = lax.broadcasted_iota(jnp.int32, (rows, lines), 1)
    one = (lax.rem(row, slots) == slot_of) & (lax.div(row, slots) == lax.rem(line, steps))
    join = jnp.sum(jnp.where(one, step_of, 0.0), axis=1, keepdims=True).astype(jnp.int32)
    later = lax.broadcasted_iota(jnp.int32, (rows, rows), 0)
    earlier = lax.broadcasted_iota(jnp.int32, (rows, rows), 1)
    t_now, t_then = lax.div(later, slots), lax.div(earlier, slots)
    kept = (lax.rem(later, slots) == lax.rem(earlier, slots)) & (t_then <= t_now)
    kept = kept & ((t_then >= join) | (t_now < join))
    scores = lax.dot_general(q_ref[...], k_ref[...], (((1,), (1,)), ((), ())), preferred_element_type=F32)
    weights = jnp.where(kept, scores * int_power(decay, t_now - t_then, steps - 1), 0.0)
    coarse = weights.astype(BF16)
    fine = (weights - coarse.astype(F32)).astype(BF16)
    v = v_ref[...]
    carried = back[:, :width].astype(BF16)
    readout = jnp.dot(jnp.where(one, 1.0, 0.0).astype(BF16), carried, preferred_element_type=F32)
    readout += jnp.dot(coarse, v, preferred_element_type=F32)
    readout += jnp.dot(fine, v, preferred_element_type=F32)
    mean = jnp.sum(readout * readout, axis=1, keepdims=True) * (1.0 / width)
    normed = readout * lax.rsqrt(mean + 1e-06) * gain_ref[...] * g_ref[...].astype(F32)
    normed = normed.astype(BF16)
    shares, _, columns = out_ref.shape
    for share in range(shares):
        part = jnp.dot(normed, w_ref[:, share * columns : (share + 1) * columns], preferred_element_type=F32)
        out_ref[HEAD_ORDER.index(share)] = part.astype(out_ref.dtype)


def total_kernel(shares_ref, out_ref):
    total = shares_ref[0].astype(F32)
    for share in range(1, shares_ref.shape[0]):
        total += shares_ref[share].astype(F32)
    out_ref[...] = total.astype(out_ref.dtype)


def call(kernel, name, out_shape, in_specs, out_specs, scratch=(), cost=None):
    return pl.pallas_call(
        kernel,
        out_shape=out_shape,
        in_specs=in_specs,
        out_specs=out_specs,
        scratch_shapes=scratch,
        compiler_params=pltpu.CompilerParams(vmem_limit_bytes=16 << 20),
        cost_estimate=cost,
        name=name,
    )


def shards(queries, keys, values, gates, prefill_states, dest_slot, arrive_step, decay, norm_gain, out_weight):
    steps, slots, key_dim = queries.shape
    val_dim = values.shape[2]
    rows = steps * slots
    per_source = dest_slot.shape[0]
    spacing = lax.axis_size("rows") // per_source
    sources, returns = [
        [[first + spacing * member for member in order] for first in range(spacing)]
        for order in (SOURCE_ORDER, RETURN_ORDER)
    ]
    shape = jax.ShapeDtypeStruct
    q = queries.reshape(rows, key_dim)
    states = prefill_states.reshape(per_source, key_dim, val_dim)
    spread, held, scale, pick, tail = call(
        lambda *refs: prepare_kernel(spacing, steps, slots, *refs),
        "spread_queries",
        (
            pltpu.VMEM((per_source, rows, key_dim), BF16),
            pltpu.VMEM(states.shape, BF16),
            pltpu.VMEM((per_source, steps, 128), F32),
            pltpu.VMEM((per_source, slots, 128), F32),
            pltpu.VMEM((per_source, steps, TAIL), F32),
        ),
        [ANY, ANY, SMEM, ANY, ANY],
        (VMEM,) * 5,
        [
            pltpu.VMEM(q.shape, BF16),
            pltpu.SMEM(dest_slot.shape, jnp.int32),
            pltpu.SMEM(arrive_step.shape, jnp.int32),
            pltpu.SemaphoreType.DMA((3 + per_source,)),
        ],
    )(in_hbm(dest_slot), in_hbm(arrive_step), decay, in_hbm(q), in_hbm(states))
    q_all = lax.all_to_all(spread, "rows", 0, 0, axis_index_groups=sources, tiled=True)
    readouts = call(
        lambda *refs: source_kernel(spacing, steps, slots, *refs),
        "source_readout",
        shape((per_source, steps, val_dim + TAIL), BF16),
        [VMEM] * 5,
        VMEM,
        cost=pl.CostEstimate(flops=2 * rows * states.size, bytes_accessed=32 << 20, transcendentals=0),
    )(q_all, held, scale, pick, tail)
    back = lax.all_to_all(readouts, "rows", 0, 0, axis_index_groups=returns, tiled=True)
    heads = lax.axis_size("heads")
    columns = out_weight.shape[1] // heads
    partial = call(
        lambda *refs: row_kernel(steps, slots, *refs),
        "combine_project",
        shape((heads, rows, columns), BF16),
        [SMEM] + [VMEM] * 7,
        VMEM,
    )(
        decay, back, q, keys.reshape(rows, key_dim), values.reshape(rows, val_dim),
        gates.reshape(rows, val_dim), norm_gain.reshape(1, val_dim), out_weight,
    )
    shares = lax.all_to_all(partial, "heads", 0, 0, axis_index_groups=[list(HEAD_ORDER)], tiled=True)
    total = call(total_kernel, "sum_heads", shape((rows, columns), BF16), [VMEM], VMEM)(shares)
    return total.reshape(steps, slots, columns)


def solution(mesh):
    placed = (
        P(None, "rows", "heads"),
        P(None, "rows", "heads"),
        P(None, "rows", "heads"),
        P(None, "rows", "heads"),
        P("rows", "heads", None, None),
        P("rows"),
        P("rows"),
        P("heads"),
        P("heads"),
        P("heads", None),
    )
    return jax.shard_map(
        shards, mesh=mesh, in_specs=placed, out_specs=P(None, "rows", "heads"), check_vma=False
    )
```

```python
import jax
import jax.numpy as jnp
from jax import lax
from jax.experimental import pallas as pl
from jax.experimental.pallas import tpu as pltpu
from jax.sharding import PartitionSpec as P

F32 = jnp.float32
BF16 = jnp.bfloat16
VMEM = pl.BlockSpec(memory_space=pltpu.VMEM)
SMEM = pl.BlockSpec(memory_space=pltpu.SMEM)
ANY = pl.BlockSpec(memory_space=pl.ANY)
TAIL = 128
SOURCE_ORDER = (5, 7, 1, 3, 4, 6, 0, 2)
RETURN_ORDER = (5, 6, 7, 0, 1, 2, 3, 4)
HEAD_ORDER = (15, 13, 14) + tuple(range(12, -1, -1))


def in_hbm(value):
    return pltpu.with_memory_space_constraint(value, pltpu.HBM)


def int_power(base, exponent, most):
    result = jnp.ones_like(exponent, dtype=F32)
    for below in range(most):
        result = jnp.where(exponent > below, result * base, result)
    return result


def prepare_kernel(
    spacing, steps, slots, dest_in, step_in, decay_ref, q_in,
    spread_ref, scale_ref, pick_ref, tail_ref, q_ref, dest_ref, step_ref, sems,
):
    peers = scale_ref.shape[0]
    first = pltpu.make_async_copy(q_in, q_ref, sems.at[0])
    ints = [
        pltpu.make_async_copy(dest_in, dest_ref, sems.at[1]),
        pltpu.make_async_copy(step_in, step_ref, sems.at[2]),
    ]
    for copy in [first] + ints:
        copy.start()
    first.wait()
    for peer in range(peers):
        spread_ref[peer] = q_ref[...]
    for copy in ints:
        copy.wait()
    member = lax.div(lax.axis_index("rows"), spacing)
    decay = decay_ref[0]
    line = lax.broadcasted_iota(jnp.int32, (steps, 128), 0)
    place = lax.broadcasted_iota(jnp.int32, (slots, 128), 0)
    lane = lax.broadcasted_iota(jnp.int32, (steps, TAIL), 1)
    for order in range(peers):
        slot = lax.rem(dest_ref[order], slots)
        joined = step_ref[order]
        age = line - joined + 1
        peer = lax.rem(member + order, peers)
        scale_ref[peer] = jnp.where(age > 0, int_power(decay, age, steps), 0.0)
        pick_ref[peer] = jnp.where(place == slot, 1.0, 0.0)
        tail_ref[peer] = jnp.where(lane < TAIL // 2, slot, joined).astype(F32)


def source_kernel(spacing, steps, slots, q_ref, state_ref, scale_ref, pick_ref, tail_ref, out_ref):
    peers, _, width = state_ref.shape
    member = lax.div(lax.axis_index("rows"), spacing)
    for block, peer in enumerate(SOURCE_ORDER):
        order = lax.rem(peer - member + peers, peers)
        full = jnp.dot(q_ref[block], state_ref[order], preferred_element_type=F32)
        scale, pick = scale_ref[peer], pick_ref[peer][None]
        parts = []
        for col in range(0, width, 128):
            part = full[:, col : col + 128].reshape(steps, slots, 128) * pick
            parts.append(jnp.sum(part, axis=1) * scale)
        parts.append(tail_ref[peer])
        out_ref[RETURN_ORDER.index(peer)] = jnp.concatenate(parts, axis=1).astype(BF16)


def row_kernel(steps, slots, decay_ref, back_ref, q_ref, k_ref, v_ref, g_ref, gain_ref, w_ref, out_ref):
    rows = steps * slots
    width = v_ref.shape[1]
    decay = decay_ref[0]
    back = back_ref[...].astype(F32)
    lines = back.shape[0] * back.shape[1]
    back = back.reshape(lines, back.shape[2])
    here = lax.broadcasted_iota(jnp.int32, (lines, TAIL), 0)
    there = lax.broadcasted_iota(jnp.int32, (lines, TAIL), 1)
    pick = here == lax.rem(there, TAIL // 2)
    facts = jnp.sum(jnp.where(pick, back[:, width:], 0.0), axis=0, keepdims=True)
    slot_of = facts[:, 0:lines].astype(jnp.int32)
    step_of = facts[:, TAIL // 2 : TAIL // 2 + lines]
    row = lax.broadcasted_iota(jnp.int32, (rows, lines), 0)
    line = lax.broadcasted_iota(jnp.int32, (rows, lines), 1)
    one = (lax.rem(row, slots) == slot_of) & (lax.div(row, slots) == lax.rem(line, steps))
    join = jnp.sum(jnp.where(one, step_of, 0.0), axis=1, keepdims=True).astype(jnp.int32)
    later = lax.broadcasted_iota(jnp.int32, (rows, rows), 0)
    earlier = lax.broadcasted_iota(jnp.int32, (rows, rows), 1)
    t_now, t_then = lax.div(later, slots), lax.div(earlier, slots)
    kept = (lax.rem(later, slots) == lax.rem(earlier, slots)) & (t_then <= t_now)
    kept = kept & ((t_then >= join) | (t_now < join))
    scores = lax.dot_general(q_ref[...], k_ref[...], (((1,), (1,)), ((), ())), preferred_element_type=F32)
    weights = jnp.where(kept, scores * int_power(decay, t_now - t_then, steps - 1), 0.0)
    coarse = weights.astype(BF16)
    fine = (weights - coarse.astype(F32)).astype(BF16)
    v = v_ref[...]
    carried = back[:, :width].astype(BF16)
    readout = jnp.dot(jnp.where(one, 1.0, 0.0).astype(BF16), carried, preferred_element_type=F32)
    readout += jnp.dot(coarse, v, preferred_element_type=F32)
    readout += jnp.dot(fine, v, preferred_element_type=F32)
    mean = jnp.sum(readout * readout, axis=1, keepdims=True) * (1.0 / width)
    normed = readout * lax.rsqrt(mean + 1e-06) * gain_ref[...] * g_ref[...].astype(F32)
    normed = normed.astype(BF16)
    shares, _, columns = out_ref.shape
    for share in range(shares):
        part = jnp.dot(normed, w_ref[:, share * columns : (share + 1) * columns], preferred_element_type=F32)
        out_ref[HEAD_ORDER.index(share)] = part.astype(out_ref.dtype)


def total_kernel(shares_ref, out_ref):
    total = shares_ref[0].astype(F32)
    for share in range(1, shares_ref.shape[0]):
        total += shares_ref[share].astype(F32)
    out_ref[...] = total.astype(out_ref.dtype)


def call(kernel, name, out_shape, in_specs, out_specs, scratch=(), cost=None):
    return pl.pallas_call(
        kernel,
        out_shape=out_shape,
        in_specs=in_specs,
        out_specs=out_specs,
        scratch_shapes=scratch,
        compiler_params=pltpu.CompilerParams(vmem_limit_bytes=16 << 20),
        cost_estimate=cost,
        name=name,
    )


def shards(queries, keys, values, gates, prefill_states, dest_slot, arrive_step, decay, norm_gain, out_weight):
    steps, slots, key_dim = queries.shape
    val_dim = values.shape[2]
    rows = steps * slots
    per_source = dest_slot.shape[0]
    spacing = lax.axis_size("rows") // per_source
    sources, returns = [
        [[first + spacing * member for member in order] for first in range(spacing)]
        for order in (SOURCE_ORDER, RETURN_ORDER)
    ]
    shape = jax.ShapeDtypeStruct
    spread_size = per_source * rows * key_dim
    q = queries.reshape(rows, key_dim)
    states = prefill_states.reshape(per_source, key_dim, val_dim)
    spread, scale, pick, tail = call(
        lambda *refs: prepare_kernel(spacing, steps, slots, *refs),
        "spread_queries",
        (
            pltpu.VMEM((per_source, rows, key_dim), BF16),
            pltpu.VMEM((per_source, steps, 128), F32),
            pltpu.VMEM((per_source, slots, 128), F32),
            pltpu.VMEM((per_source, steps, TAIL), F32),
        ),
        [ANY, ANY, SMEM, ANY],
        (VMEM,) * 4,
        [
            pltpu.VMEM(q.shape, BF16),
            pltpu.SMEM(dest_slot.shape, jnp.int32),
            pltpu.SMEM(arrive_step.shape, jnp.int32),
            pltpu.SemaphoreType.DMA((3,)),
        ],
        pl.CostEstimate(flops=20 * 10**9, bytes_accessed=2 * spread_size, transcendentals=0),
    )(in_hbm(dest_slot), in_hbm(arrive_step), decay, in_hbm(q))
    q_all = lax.all_to_all(spread, "rows", 0, 0, axis_index_groups=sources, tiled=True)
    readouts = call(
        lambda *refs: source_kernel(spacing, steps, slots, *refs),
        "source_readout",
        shape((per_source, steps, val_dim + TAIL), BF16),
        [VMEM] * 5,
        VMEM,
        cost=pl.CostEstimate(flops=20 * 10**9, bytes_accessed=2 * states.size, transcendentals=0),
    )(q_all, states, scale, pick, tail)
    back = lax.all_to_all(readouts, "rows", 0, 0, axis_index_groups=returns, tiled=True)
    heads = lax.axis_size("heads")
    columns = out_weight.shape[1] // heads
    partial = call(
        lambda *refs: row_kernel(steps, slots, *refs),
        "combine_project",
        shape((heads, rows, columns), BF16),
        [SMEM] + [VMEM] * 7,
        VMEM,
    )(
        decay, back, q, keys.reshape(rows, key_dim), values.reshape(rows, val_dim),
        gates.reshape(rows, val_dim), norm_gain.reshape(1, val_dim), out_weight,
    )
    shares = lax.all_to_all(partial, "heads", 0, 0, axis_index_groups=[list(HEAD_ORDER)], tiled=True)
    total = call(total_kernel, "sum_heads", shape((rows, columns), BF16), [VMEM], VMEM)(shares)
    return total.reshape(steps, slots, columns)


def solution(mesh):
    placed = (
        P(None, "rows", "heads"),
        P(None, "rows", "heads"),
        P(None, "rows", "heads"),
        P(None, "rows", "heads"),
        P("rows", "heads", None, None),
        P("rows"),
        P("rows"),
        P("heads"),
        P("heads"),
        P("heads", None),
    )
    return jax.shard_map(
        shards, mesh=mesh, in_specs=placed, out_specs=P(None, "rows", "heads"), check_vma=False
    )
```

```python
import jax
import jax.numpy as jnp
from jax import lax
from jax.experimental import pallas as pl
from jax.experimental.pallas import tpu as pltpu
from jax.sharding import PartitionSpec as P

F32 = jnp.float32
BF16 = jnp.bfloat16
VMEM = pl.BlockSpec(memory_space=pltpu.VMEM)
SMEM = pl.BlockSpec(memory_space=pltpu.SMEM)
ANY = pl.BlockSpec(memory_space=pl.ANY)
TAIL = 128
SOURCE_ORDER = (5, 7, 1, 3, 4, 6, 0, 2)
RETURN_ORDER = (5, 6, 7, 0, 1, 2, 3, 4)
HEAD_ORDER = (15, 13, 14, 10, 12, 8, 11, 6, 9, 4, 7, 2, 5, 1, 3, 0)


def in_hbm(value):
    return pltpu.with_memory_space_constraint(value, pltpu.HBM)


def int_power(base, exponent, most):
    result = jnp.ones_like(exponent, dtype=F32)
    for below in range(most):
        result = jnp.where(exponent > below, result * base, result)
    return result


def prepare_kernel(
    spacing, steps, slots, dest_in, step_in, decay_ref, q_in,
    spread_ref, scale_ref, pick_ref, tail_ref, q_ref, dest_ref, step_ref, sems,
):
    peers = scale_ref.shape[0]
    first = pltpu.make_async_copy(q_in, q_ref, sems.at[0])
    ints = [
        pltpu.make_async_copy(dest_in, dest_ref, sems.at[1]),
        pltpu.make_async_copy(step_in, step_ref, sems.at[2]),
    ]
    for copy in [first] + ints:
        copy.start()
    first.wait()
    for peer in range(peers):
        spread_ref[peer] = q_ref[...]
    for copy in ints:
        copy.wait()
    member = lax.div(lax.axis_index("rows"), spacing)
    decay = decay_ref[0]
    line = lax.broadcasted_iota(jnp.int32, (steps, 128), 0)
    place = lax.broadcasted_iota(jnp.int32, (slots, 128), 0)
    lane = lax.broadcasted_iota(jnp.int32, (steps, TAIL), 1)
    for order in range(peers):
        slot = lax.rem(dest_ref[order], slots)
        joined = step_ref[order]
        age = line - joined + 1
        peer = lax.rem(member + order, peers)
        scale_ref[peer] = jnp.where(age > 0, int_power(decay, age, steps), 0.0)
        pick_ref[peer] = jnp.where(place == slot, 1.0, 0.0)
        tail_ref[peer] = jnp.where(lane < TAIL // 2, slot, joined).astype(F32)


def source_kernel(spacing, steps, slots, q_ref, state_ref, scale_ref, pick_ref, tail_ref, out_ref):
    peers, _, width = state_ref.shape
    member = lax.div(lax.axis_index("rows"), spacing)
    for block, peer in enumerate(SOURCE_ORDER):
        order = lax.rem(peer - member + peers, peers)
        full = jnp.dot(q_ref[block], state_ref[order], preferred_element_type=F32)
        scale, pick = scale_ref[peer], pick_ref[peer][None]
        parts = []
        for col in range(0, width, 128):
            part = full[:, col : col + 128].reshape(steps, slots, 128) * pick
            parts.append(jnp.sum(part, axis=1) * scale)
        parts.append(tail_ref[peer])
        out_ref[RETURN_ORDER.index(peer)] = jnp.concatenate(parts, axis=1).astype(BF16)


def row_kernel(steps, slots, decay_ref, back_ref, q_ref, k_ref, v_ref, g_ref, gain_ref, w_ref, out_ref):
    rows = steps * slots
    width = v_ref.shape[1]
    decay = decay_ref[0]
    back = back_ref[...].astype(F32)
    lines = back.shape[0] * back.shape[1]
    back = back.reshape(lines, back.shape[2])
    here = lax.broadcasted_iota(jnp.int32, (lines, TAIL), 0)
    there = lax.broadcasted_iota(jnp.int32, (lines, TAIL), 1)
    pick = here == lax.rem(there, TAIL // 2)
    facts = jnp.sum(jnp.where(pick, back[:, width:], 0.0), axis=0, keepdims=True)
    slot_of = facts[:, 0:lines].astype(jnp.int32)
    step_of = facts[:, TAIL // 2 : TAIL // 2 + lines]
    row = lax.broadcasted_iota(jnp.int32, (rows, lines), 0)
    line = lax.broadcasted_iota(jnp.int32, (rows, lines), 1)
    one = (lax.rem(row, slots) == slot_of) & (lax.div(row, slots) == lax.rem(line, steps))
    join = jnp.sum(jnp.where(one, step_of, 0.0), axis=1, keepdims=True).astype(jnp.int32)
    later = lax.broadcasted_iota(jnp.int32, (rows, rows), 0)
    earlier = lax.broadcasted_iota(jnp.int32, (rows, rows), 1)
    t_now, t_then = lax.div(later, slots), lax.div(earlier, slots)
    kept = (lax.rem(later, slots) == lax.rem(earlier, slots)) & (t_then <= t_now)
    kept = kept & ((t_then >= join) | (t_now < join))
    scores = lax.dot_general(q_ref[...], k_ref[...], (((1,), (1,)), ((), ())), preferred_element_type=F32)
    weights = jnp.where(kept, scores * int_power(decay, t_now - t_then, steps - 1), 0.0)
    coarse = weights.astype(BF16)
    fine = (weights - coarse.astype(F32)).astype(BF16)
    v = v_ref[...]
    carried = back[:, :width].astype(BF16)
    readout = jnp.dot(jnp.where(one, 1.0, 0.0).astype(BF16), carried, preferred_element_type=F32)
    readout += jnp.dot(coarse, v, preferred_element_type=F32)
    readout += jnp.dot(fine, v, preferred_element_type=F32)
    mean = jnp.sum(readout * readout, axis=1, keepdims=True) * (1.0 / width)
    normed = readout * lax.rsqrt(mean + 1e-06) * gain_ref[...] * g_ref[...].astype(F32)
    normed = normed.astype(BF16)
    shares, _, columns = out_ref.shape
    for share in range(shares):
        part = jnp.dot(normed, w_ref[:, share * columns : (share + 1) * columns], preferred_element_type=F32)
        out_ref[HEAD_ORDER.index(share)] = part.astype(out_ref.dtype)


def total_kernel(shares_ref, out_ref):
    total = shares_ref[0].astype(F32)
    for share in range(1, shares_ref.shape[0]):
        total += shares_ref[share].astype(F32)
    out_ref[...] = total.astype(out_ref.dtype)


def call(kernel, name, out_shape, in_specs, out_specs, scratch=(), cost=None):
    return pl.pallas_call(
        kernel,
        out_shape=out_shape,
        in_specs=in_specs,
        out_specs=out_specs,
        scratch_shapes=scratch,
        compiler_params=pltpu.CompilerParams(vmem_limit_bytes=16 << 20),
        cost_estimate=cost,
        name=name,
    )


def shards(queries, keys, values, gates, prefill_states, dest_slot, arrive_step, decay, norm_gain, out_weight):
    steps, slots, key_dim = queries.shape
    val_dim = values.shape[2]
    rows = steps * slots
    per_source = dest_slot.shape[0]
    spacing = lax.axis_size("rows") // per_source
    sources, returns = [
        [[first + spacing * member for member in order] for first in range(spacing)]
        for order in (SOURCE_ORDER, RETURN_ORDER)
    ]
    shape = jax.ShapeDtypeStruct
    spread_size = per_source * rows * key_dim
    q = queries.reshape(rows, key_dim)
    states = prefill_states.reshape(per_source, key_dim, val_dim)
    spread, scale, pick, tail = call(
        lambda *refs: prepare_kernel(spacing, steps, slots, *refs),
        "spread_queries",
        (
            pltpu.VMEM((per_source, rows, key_dim), BF16),
            pltpu.VMEM((per_source, steps, 128), F32),
            pltpu.VMEM((per_source, slots, 128), F32),
            pltpu.VMEM((per_source, steps, TAIL), F32),
        ),
        [ANY, ANY, SMEM, ANY],
        (VMEM,) * 4,
        [
            pltpu.VMEM(q.shape, BF16),
            pltpu.SMEM(dest_slot.shape, jnp.int32),
            pltpu.SMEM(arrive_step.shape, jnp.int32),
            pltpu.SemaphoreType.DMA((3,)),
        ],
        pl.CostEstimate(flops=20 * 10**9, bytes_accessed=2 * spread_size, transcendentals=0),
    )(in_hbm(dest_slot), in_hbm(arrive_step), decay, in_hbm(q))
    q_all = lax.all_to_all(spread, "rows", 0, 0, axis_index_groups=sources, tiled=True)
    readouts = call(
        lambda *refs: source_kernel(spacing, steps, slots, *refs),
        "source_readout",
        shape((per_source, steps, val_dim + TAIL), BF16),
        [VMEM] * 5,
        VMEM,
        cost=pl.CostEstimate(flops=20 * 10**9, bytes_accessed=2 * states.size, transcendentals=0),
    )(q_all, states, scale, pick, tail)
    back = lax.all_to_all(readouts, "rows", 0, 0, axis_index_groups=returns, tiled=True)
    heads = lax.axis_size("heads")
    columns = out_weight.shape[1] // heads
    partial = call(
        lambda *refs: row_kernel(steps, slots, *refs),
        "combine_project",
        shape((heads, rows, columns), BF16),
        [SMEM] + [VMEM] * 7,
        VMEM,
    )(
        decay, back, q, keys.reshape(rows, key_dim), values.reshape(rows, val_dim),
        gates.reshape(rows, val_dim), norm_gain.reshape(1, val_dim), out_weight,
    )
    shares = lax.all_to_all(partial, "heads", 0, 0, axis_index_groups=[list(HEAD_ORDER)], tiled=True)
    total = call(total_kernel, "sum_heads", shape((rows, columns), BF16), [VMEM], VMEM)(shares)
    return total.reshape(steps, slots, columns)


def solution(mesh):
    placed = (
        P(None, "rows", "heads"),
        P(None, "rows", "heads"),
        P(None, "rows", "heads"),
        P(None, "rows", "heads"),
        P("rows", "heads", None, None),
        P("rows"),
        P("rows"),
        P("heads"),
        P("heads"),
        P("heads", None),
    )
    return jax.shard_map(
        shards, mesh=mesh, in_specs=placed, out_specs=P(None, "rows", "heads"), check_vma=False
    )
```

```python
import jax
import jax.numpy as jnp
from jax import lax
from jax.experimental import pallas as pl
from jax.experimental.pallas import tpu as pltpu
from jax.sharding import PartitionSpec as P

F32 = jnp.float32
BF16 = jnp.bfloat16
VMEM = pl.BlockSpec(memory_space=pltpu.VMEM)
SMEM = pl.BlockSpec(memory_space=pltpu.SMEM)
ANY = pl.BlockSpec(memory_space=pl.ANY)
TAIL = 128
SOURCE_ORDER = (5, 7, 1, 3, 4, 6, 0, 2)
RETURN_ORDER = (5, 6, 7, 0, 1, 2, 3, 4)
HEAD_ORDER = (15, 13, 14, 10, 12, 8, 11, 6, 9, 4, 7, 2, 5, 1, 3, 0)


def in_hbm(value):
    return pltpu.with_memory_space_constraint(value, pltpu.HBM)


def int_power(base, exponent, most):
    result = jnp.ones_like(exponent, dtype=F32)
    for below in range(most):
        result = jnp.where(exponent > below, result * base, result)
    return result


def prepare_kernel(
    spacing, steps, slots, dest_in, step_in, decay_ref, q_in,
    spread_ref, scale_ref, pick_ref, tail_ref, q_ref, dest_ref, step_ref, sems,
):
    peers = scale_ref.shape[0]
    first = pltpu.make_async_copy(q_in, q_ref, sems.at[0])
    ints = [
        pltpu.make_async_copy(dest_in, dest_ref, sems.at[1]),
        pltpu.make_async_copy(step_in, step_ref, sems.at[2]),
    ]
    for copy in [first] + ints:
        copy.start()
    first.wait()
    for peer in range(peers):
        spread_ref[peer] = q_ref[...]
    for copy in ints:
        copy.wait()
    member = lax.div(lax.axis_index("rows"), spacing)
    decay = decay_ref[0]
    line = lax.broadcasted_iota(jnp.int32, (steps, 128), 0)
    place = lax.broadcasted_iota(jnp.int32, (slots, 128), 0)
    lane = lax.broadcasted_iota(jnp.int32, (steps, TAIL), 1)
    for order in range(peers):
        slot = lax.rem(dest_ref[order], slots)
        joined = step_ref[order]
        age = line - joined + 1
        peer = lax.rem(member + order, peers)
        scale_ref[peer] = jnp.where(age > 0, int_power(decay, age, steps), 0.0)
        pick_ref[peer] = jnp.where(place == slot, 1.0, 0.0)
        tail_ref[peer] = jnp.where(lane < TAIL // 2, slot, joined).astype(F32)


def source_kernel(spacing, steps, slots, q_ref, state_ref, scale_ref, pick_ref, tail_ref, out_ref):
    peers, _, width = state_ref.shape
    member = lax.div(lax.axis_index("rows"), spacing)
    for block, peer in enumerate(SOURCE_ORDER):
        order = lax.rem(peer - member + peers, peers)
        full = jnp.dot(q_ref[block], state_ref[order], preferred_element_type=F32)
        scale, pick = scale_ref[peer], pick_ref[peer][None]
        parts = []
        for col in range(0, width, 128):
            part = full[:, col : col + 128].reshape(steps, slots, 128) * pick
            parts.append(jnp.sum(part, axis=1) * scale)
        parts.append(tail_ref[peer])
        out_ref[RETURN_ORDER.index(peer)] = jnp.concatenate(parts, axis=1).astype(BF16)


def row_kernel(steps, slots, decay_ref, back_ref, q_ref, k_ref, v_ref, g_ref, gain_ref, w_ref, out_ref):
    rows = steps * slots
    width = v_ref.shape[1]
    decay = decay_ref[0]
    back = back_ref[...].astype(F32)
    lines = back.shape[0] * back.shape[1]
    back = back.reshape(lines, back.shape[2])
    here = lax.broadcasted_iota(jnp.int32, (lines, TAIL), 0)
    there = lax.broadcasted_iota(jnp.int32, (lines, TAIL), 1)
    pick = here == lax.rem(there, TAIL // 2)
    facts = jnp.sum(jnp.where(pick, back[:, width:], 0.0), axis=0, keepdims=True)
    slot_of = facts[:, 0:lines].astype(jnp.int32)
    step_of = facts[:, TAIL // 2 : TAIL // 2 + lines]
    row = lax.broadcasted_iota(jnp.int32, (rows, lines), 0)
    line = lax.broadcasted_iota(jnp.int32, (rows, lines), 1)
    one = (lax.rem(row, slots) == slot_of) & (lax.div(row, slots) == lax.rem(line, steps))
    join = jnp.sum(jnp.where(one, step_of, 0.0), axis=1, keepdims=True).astype(jnp.int32)
    later = lax.broadcasted_iota(jnp.int32, (rows, rows), 0)
    earlier = lax.broadcasted_iota(jnp.int32, (rows, rows), 1)
    t_now, t_then = lax.div(later, slots), lax.div(earlier, slots)
    kept = (lax.rem(later, slots) == lax.rem(earlier, slots)) & (t_then <= t_now)
    kept = kept & ((t_then >= join) | (t_now < join))
    scores = lax.dot_general(q_ref[...], k_ref[...], (((1,), (1,)), ((), ())), preferred_element_type=F32)
    weights = jnp.where(kept, scores * int_power(decay, t_now - t_then, steps - 1), 0.0)
    coarse = weights.astype(BF16)
    fine = (weights - coarse.astype(F32)).astype(BF16)
    v = v_ref[...]
    carried = back[:, :width].astype(BF16)
    left = jnp.concatenate([jnp.where(one, 1.0, 0.0).astype(BF16), coarse, fine], axis=1)
    right = jnp.concatenate([carried, v, v], axis=0)
    readout = jnp.dot(left, right, preferred_element_type=F32)
    mean = jnp.sum(readout * readout, axis=1, keepdims=True) * (1.0 / width)
    normed = readout * lax.rsqrt(mean + 1e-06) * gain_ref[...] * g_ref[...].astype(F32)
    normed = normed.astype(BF16)
    shares, _, columns = out_ref.shape
    for share in range(0, shares, 2):
        part = jnp.dot(normed, w_ref[:, share * columns : (share + 2) * columns], preferred_element_type=F32)
        part = part.astype(out_ref.dtype)
        out_ref[HEAD_ORDER.index(share)] = part[:, 0:columns]
        out_ref[HEAD_ORDER.index(share + 1)] = part[:, columns:]


def total_kernel(shares_ref, out_ref):
    total = shares_ref[0].astype(F32)
    for share in range(1, shares_ref.shape[0]):
        total += shares_ref[share].astype(F32)
    out_ref[...] = total.astype(out_ref.dtype)


def call(kernel, name, out_shape, in_specs, out_specs, scratch=(), cost=None):
    return pl.pallas_call(
        kernel,
        out_shape=out_shape,
        in_specs=in_specs,
        out_specs=out_specs,
        scratch_shapes=scratch,
        compiler_params=pltpu.CompilerParams(vmem_limit_bytes=16 << 20),
        cost_estimate=cost,
        name=name,
    )


def shards(queries, keys, values, gates, prefill_states, dest_slot, arrive_step, decay, norm_gain, out_weight):
    steps, slots, key_dim = queries.shape
    val_dim = values.shape[2]
    rows = steps * slots
    per_source = dest_slot.shape[0]
    spacing = lax.axis_size("rows") // per_source
    sources, returns = [
        [[first + spacing * member for member in order] for first in range(spacing)]
        for order in (SOURCE_ORDER, RETURN_ORDER)
    ]
    shape = jax.ShapeDtypeStruct
    spread_size = per_source * rows * key_dim
    q = queries.reshape(rows, key_dim)
    states = prefill_states.reshape(per_source, key_dim, val_dim)
    spread, scale, pick, tail = call(
        lambda *refs: prepare_kernel(spacing, steps, slots, *refs),
        "spread_queries",
        (
            pltpu.VMEM((per_source, rows, key_dim), BF16),
            pltpu.VMEM((per_source, steps, 128), F32),
            pltpu.VMEM((per_source, slots, 128), F32),
            pltpu.VMEM((per_source, steps, TAIL), F32),
        ),
        [ANY, ANY, SMEM, ANY],
        (VMEM,) * 4,
        [
            pltpu.VMEM(q.shape, BF16),
            pltpu.SMEM(dest_slot.shape, jnp.int32),
            pltpu.SMEM(arrive_step.shape, jnp.int32),
            pltpu.SemaphoreType.DMA((3,)),
        ],
        pl.CostEstimate(flops=20 * 10**9, bytes_accessed=2 * spread_size, transcendentals=0),
    )(in_hbm(dest_slot), in_hbm(arrive_step), decay, in_hbm(q))
    q_all = lax.all_to_all(spread, "rows", 0, 0, axis_index_groups=sources, tiled=True)
    readouts = call(
        lambda *refs: source_kernel(spacing, steps, slots, *refs),
        "source_readout",
        shape((per_source, steps, val_dim + TAIL), BF16),
        [VMEM] * 5,
        VMEM,
        cost=pl.CostEstimate(flops=20 * 10**9, bytes_accessed=2 * states.size, transcendentals=0),
    )(q_all, states, scale, pick, tail)
    back = lax.all_to_all(readouts, "rows", 0, 0, axis_index_groups=returns, tiled=True)
    heads = lax.axis_size("heads")
    columns = out_weight.shape[1] // heads
    partial = call(
        lambda *refs: row_kernel(steps, slots, *refs),
        "combine_project",
        shape((heads, rows, columns), BF16),
        [SMEM] + [VMEM] * 7,
        VMEM,
    )(
        decay, back, q, keys.reshape(rows, key_dim), values.reshape(rows, val_dim),
        gates.reshape(rows, val_dim), norm_gain.reshape(1, val_dim), out_weight,
    )
    shares = lax.all_to_all(partial, "heads", 0, 0, axis_index_groups=[list(HEAD_ORDER)], tiled=True)
    total = call(total_kernel, "sum_heads", shape((rows, columns), BF16), [VMEM], VMEM)(shares)
    return total.reshape(steps, slots, columns)


def solution(mesh):
    placed = (
        P(None, "rows", "heads"),
        P(None, "rows", "heads"),
        P(None, "rows", "heads"),
        P(None, "rows", "heads"),
        P("rows", "heads", None, None),
        P("rows"),
        P("rows"),
        P("heads"),
        P("heads"),
        P("heads", None),
    )
    return jax.shard_map(
        shards, mesh=mesh, in_specs=placed, out_specs=P(None, "rows", "heads"), check_vma=False
    )
```

```python
import jax
import jax.numpy as jnp
from jax import lax
from jax.experimental import pallas as pl
from jax.experimental.pallas import tpu as pltpu
from jax.sharding import PartitionSpec as P

F32 = jnp.float32
BF16 = jnp.bfloat16
VMEM = pl.BlockSpec(memory_space=pltpu.VMEM)
SMEM = pl.BlockSpec(memory_space=pltpu.SMEM)
ANY = pl.BlockSpec(memory_space=pl.ANY)
TAIL = 128
SOURCE_ORDER = (5, 7, 1, 3, 4, 6, 0, 2)
RETURN_ORDER = (5, 6, 7, 0, 1, 2, 3, 4)
HEAD_ORDER = (15, 13, 14, 10, 12, 8, 11, 6, 9, 4, 7, 2, 5, 1, 3, 0)


def in_hbm(value):
    return pltpu.with_memory_space_constraint(value, pltpu.HBM)


def int_power(base, exponent, most):
    result = jnp.ones_like(exponent, dtype=F32)
    for below in range(most):
        result = jnp.where(exponent > below, result * base, result)
    return result


def prepare_kernel(
    spacing, steps, slots, dest_in, step_in, decay_ref, q_in,
    spread_ref, scale_ref, pick_ref, tail_ref, dest_ref, step_ref, sems,
):
    peers = scale_ref.shape[0]
    first = pltpu.make_async_copy(q_in, spread_ref.at[0], sems.at[0])
    ints = [
        pltpu.make_async_copy(dest_in, dest_ref, sems.at[1]),
        pltpu.make_async_copy(step_in, step_ref, sems.at[2]),
    ]
    for copy in [first] + ints:
        copy.start()
    first.wait()
    own = spread_ref[0]
    for peer in range(1, peers):
        spread_ref[peer] = own
    for copy in ints:
        copy.wait()
    member = lax.div(lax.axis_index("rows"), spacing)
    decay = decay_ref[0]
    line = lax.broadcasted_iota(jnp.int32, (steps, 128), 0)
    place = lax.broadcasted_iota(jnp.int32, (slots, 128), 0)
    lane = lax.broadcasted_iota(jnp.int32, (steps, TAIL), 1)
    for order in range(peers):
        slot = lax.rem(dest_ref[order], slots)
        joined = step_ref[order]
        age = line - joined + 1
        peer = lax.rem(member + order, peers)
        scale_ref[peer] = jnp.where(age > 0, int_power(decay, age, steps), 0.0)
        pick_ref[peer] = jnp.where(place == slot, 1.0, 0.0)
        tail_ref[peer] = jnp.where(lane < TAIL // 2, slot, joined).astype(F32)


def source_kernel(spacing, steps, slots, q_ref, state_ref, scale_ref, pick_ref, tail_ref, out_ref):
    peers, _, width = state_ref.shape
    member = lax.div(lax.axis_index("rows"), spacing)
    for block, peer in enumerate(SOURCE_ORDER):
        order = lax.rem(peer - member + peers, peers)
        full = jnp.dot(q_ref[block], state_ref[order], preferred_element_type=F32)
        scale, pick = scale_ref[peer], pick_ref[peer][None]
        parts = []
        for col in range(0, width, 128):
            part = full[:, col : col + 128].reshape(steps, slots, 128) * pick
            parts.append(jnp.sum(part, axis=1) * scale)
        parts.append(tail_ref[peer])
        out_ref[RETURN_ORDER.index(peer)] = jnp.concatenate(parts, axis=1).astype(BF16)


def row_kernel(steps, slots, decay_ref, back_ref, q_ref, k_ref, v_ref, g_ref, gain_ref, w_ref, out_ref):
    rows = steps * slots
    width = v_ref.shape[1]
    decay = decay_ref[0]
    back = back_ref[...].astype(F32)
    lines = back.shape[0] * back.shape[1]
    back = back.reshape(lines, back.shape[2])
    here = lax.broadcasted_iota(jnp.int32, (lines, TAIL), 0)
    there = lax.broadcasted_iota(jnp.int32, (lines, TAIL), 1)
    pick = here == lax.rem(there, TAIL // 2)
    facts = jnp.sum(jnp.where(pick, back[:, width:], 0.0), axis=0, keepdims=True)
    slot_of = facts[:, 0:lines].astype(jnp.int32)
    step_of = facts[:, TAIL // 2 : TAIL // 2 + lines]
    row = lax.broadcasted_iota(jnp.int32, (rows, lines), 0)
    line = lax.broadcasted_iota(jnp.int32, (rows, lines), 1)
    one = (lax.rem(row, slots) == slot_of) & (lax.div(row, slots) == lax.rem(line, steps))
    join = jnp.sum(jnp.where(one, step_of, 0.0), axis=1, keepdims=True).astype(jnp.int32)
    later = lax.broadcasted_iota(jnp.int32, (rows, rows), 0)
    earlier = lax.broadcasted_iota(jnp.int32, (rows, rows), 1)
    t_now, t_then = lax.div(later, slots), lax.div(earlier, slots)
    kept = (lax.rem(later, slots) == lax.rem(earlier, slots)) & (t_then <= t_now)
    kept = kept & ((t_then >= join) | (t_now < join))
    scores = lax.dot_general(q_ref[...], k_ref[...], (((1,), (1,)), ((), ())), preferred_element_type=F32)
    weights = jnp.where(kept, scores * int_power(decay, t_now - t_then, steps - 1), 0.0)
    coarse = weights.astype(BF16)
    fine = (weights - coarse.astype(F32)).astype(BF16)
    v = v_ref[...]
    carried = back[:, :width].astype(BF16)
    left = jnp.concatenate([jnp.where(one, 1.0, 0.0).astype(BF16), coarse, fine], axis=1)
    right = jnp.concatenate([carried, v, v], axis=0)
    readout = jnp.dot(left, right, preferred_element_type=F32)
    mean = jnp.sum(readout * readout, axis=1, keepdims=True) * (1.0 / width)
    normed = readout * lax.rsqrt(mean + 1e-06) * gain_ref[...] * g_ref[...].astype(F32)
    normed = normed.astype(BF16)
    shares, _, columns = out_ref.shape
    for share in range(0, shares, 2):
        part = jnp.dot(normed, w_ref[:, share * columns : (share + 2) * columns], preferred_element_type=F32)
        part = part.astype(out_ref.dtype)
        out_ref[HEAD_ORDER.index(share)] = part[:, 0:columns]
        out_ref[HEAD_ORDER.index(share + 1)] = part[:, columns:]


def total_kernel(shares_ref, out_ref):
    total = shares_ref[0].astype(F32)
    for share in range(1, shares_ref.shape[0]):
        total += shares_ref[share].astype(F32)
    out_ref[...] = total.astype(out_ref.dtype)


def call(kernel, name, out_shape, in_specs, out_specs, scratch=(), cost=None):
    return pl.pallas_call(
        kernel,
        out_shape=out_shape,
        in_specs=in_specs,
        out_specs=out_specs,
        scratch_shapes=scratch,
        compiler_params=pltpu.CompilerParams(vmem_limit_bytes=16 << 20),
        cost_estimate=cost,
        name=name,
    )


def shards(queries, keys, values, gates, prefill_states, dest_slot, arrive_step, decay, norm_gain, out_weight):
    steps, slots, key_dim = queries.shape
    val_dim = values.shape[2]
    rows = steps * slots
    per_source = dest_slot.shape[0]
    spacing = lax.axis_size("rows") // per_source
    sources, returns = [
        [[first + spacing * member for member in order] for first in range(spacing)]
        for order in (SOURCE_ORDER, RETURN_ORDER)
    ]
    shape = jax.ShapeDtypeStruct
    spread_size = per_source * rows * key_dim
    q = queries.reshape(rows, key_dim)
    states = prefill_states.reshape(per_source, key_dim, val_dim)
    spread, scale, pick, tail = call(
        lambda *refs: prepare_kernel(spacing, steps, slots, *refs),
        "spread_queries",
        (
            pltpu.VMEM((per_source, rows, key_dim), BF16),
            pltpu.VMEM((per_source, steps, 128), F32),
            pltpu.VMEM((per_source, slots, 128), F32),
            pltpu.VMEM((per_source, steps, TAIL), F32),
        ),
        [ANY, ANY, SMEM, ANY],
        (VMEM,) * 4,
        [
            pltpu.SMEM(dest_slot.shape, jnp.int32),
            pltpu.SMEM(arrive_step.shape, jnp.int32),
            pltpu.SemaphoreType.DMA((3,)),
        ],
        pl.CostEstimate(flops=20 * 10**9, bytes_accessed=2 * spread_size, transcendentals=0),
    )(in_hbm(dest_slot), in_hbm(arrive_step), decay, in_hbm(q))
    q_all = lax.all_to_all(spread, "rows", 0, 0, axis_index_groups=sources, tiled=True)
    readouts = call(
        lambda *refs: source_kernel(spacing, steps, slots, *refs),
        "source_readout",
        shape((per_source, steps, val_dim + TAIL), BF16),
        [VMEM] * 5,
        VMEM,
        cost=pl.CostEstimate(flops=20 * 10**9, bytes_accessed=2 * states.size, transcendentals=0),
    )(q_all, states, scale, pick, tail)
    back = lax.all_to_all(readouts, "rows", 0, 0, axis_index_groups=returns, tiled=True)
    heads = lax.axis_size("heads")
    columns = out_weight.shape[1] // heads
    partial = call(
        lambda *refs: row_kernel(steps, slots, *refs),
        "combine_project",
        shape((heads, rows, columns), BF16),
        [SMEM] + [VMEM] * 7,
        VMEM,
    )(
        decay, back, q, keys.reshape(rows, key_dim), values.reshape(rows, val_dim),
        gates.reshape(rows, val_dim), norm_gain.reshape(1, val_dim), out_weight,
    )
    shares = lax.all_to_all(partial, "heads", 0, 0, axis_index_groups=[list(HEAD_ORDER)], tiled=True)
    total = call(total_kernel, "sum_heads", shape((rows, columns), BF16), [VMEM], VMEM)(shares)
    return total.reshape(steps, slots, columns)


def solution(mesh):
    placed = (
        P(None, "rows", "heads"),
        P(None, "rows", "heads"),
        P(None, "rows", "heads"),
        P(None, "rows", "heads"),
        P("rows", "heads", None, None),
        P("rows"),
        P("rows"),
        P("heads"),
        P("heads"),
        P("heads", None),
    )
    return jax.shard_map(
        shards, mesh=mesh, in_specs=placed, out_specs=P(None, "rows", "heads"), check_vma=False
    )
```

```python
import jax
import jax.numpy as jnp
from jax import lax
from jax.experimental import pallas as pl
from jax.experimental.pallas import tpu as pltpu
from jax.sharding import PartitionSpec as P

F32 = jnp.float32
BF16 = jnp.bfloat16
VMEM = pl.BlockSpec(memory_space=pltpu.VMEM)
SMEM = pl.BlockSpec(memory_space=pltpu.SMEM)
ANY = pl.BlockSpec(memory_space=pl.ANY)
TAIL = 128
SOURCE_ORDER = (5, 7, 1, 3, 4, 6, 0, 2)
RETURN_ORDER = (5, 6, 7, 0, 1, 2, 3, 4)
HEAD_ORDER = (15, 12, 14, 10, 13, 8, 11, 6, 9, 4, 7, 2, 5, 0, 3, 1)


def in_hbm(value):
    return pltpu.with_memory_space_constraint(value, pltpu.HBM)


def int_power(base, exponent, most):
    result = jnp.ones_like(exponent, dtype=F32)
    for below in range(most):
        result = jnp.where(exponent > below, result * base, result)
    return result


def prepare_kernel(
    spacing, steps, slots, dest_in, step_in, decay_ref, q_in,
    spread_ref, scale_ref, pick_ref, tail_ref, dest_ref, step_ref, sems,
):
    peers = scale_ref.shape[0]
    first = pltpu.make_async_copy(q_in, spread_ref.at[0], sems.at[0])
    ints = [
        pltpu.make_async_copy(dest_in, dest_ref, sems.at[1]),
        pltpu.make_async_copy(step_in, step_ref, sems.at[2]),
    ]
    for copy in [first] + ints:
        copy.start()
    first.wait()
    own = spread_ref[0]
    for peer in range(1, peers):
        spread_ref[peer] = own
    for copy in ints:
        copy.wait()
    member = lax.div(lax.axis_index("rows"), spacing)
    decay = decay_ref[0]
    line = lax.broadcasted_iota(jnp.int32, (steps, 128), 0)
    place = lax.broadcasted_iota(jnp.int32, (slots, 128), 0)
    lane = lax.broadcasted_iota(jnp.int32, (steps, TAIL), 1)
    for order in range(peers):
        slot = lax.rem(dest_ref[order], slots)
        joined = step_ref[order]
        age = line - joined + 1
        peer = lax.rem(member + order, peers)
        scale_ref[peer] = jnp.where(age > 0, int_power(decay, age, steps), 0.0)
        pick_ref[peer] = jnp.where(place == slot, 1.0, 0.0)
        tail_ref[peer] = jnp.where(lane < TAIL // 2, slot, joined).astype(F32)


def source_kernel(spacing, steps, slots, q_ref, state_ref, scale_ref, pick_ref, tail_ref, out_ref):
    peers, _, width = state_ref.shape
    member = lax.div(lax.axis_index("rows"), spacing)
    for block, peer in enumerate(SOURCE_ORDER):
        order = lax.rem(peer - member + peers, peers)
        full = jnp.dot(q_ref[block], state_ref[order], preferred_element_type=F32)
        scale, pick = scale_ref[peer], pick_ref[peer][None]
        parts = []
        for col in range(0, width, 128):
            part = full[:, col : col + 128].reshape(steps, slots, 128) * pick
            parts.append(jnp.sum(part, axis=1) * scale)
        parts.append(tail_ref[peer])
        out_ref[RETURN_ORDER.index(peer)] = jnp.concatenate(parts, axis=1).astype(BF16)


def row_kernel(steps, slots, decay_ref, back_ref, q_ref, k_ref, v_ref, g_ref, gain_ref, w_ref, out_ref):
    rows = steps * slots
    width = v_ref.shape[1]
    decay = decay_ref[0]
    back = back_ref[...].astype(F32)
    lines = back.shape[0] * back.shape[1]
    back = back.reshape(lines, back.shape[2])
    here = lax.broadcasted_iota(jnp.int32, (lines, TAIL), 0)
    there = lax.broadcasted_iota(jnp.int32, (lines, TAIL), 1)
    pick = here == lax.rem(there, TAIL // 2)
    facts = jnp.sum(jnp.where(pick, back[:, width:], 0.0), axis=0, keepdims=True)
    slot_of = facts[:, 0:lines].astype(jnp.int32)
    step_of = facts[:, TAIL // 2 : TAIL // 2 + lines]
    row = lax.broadcasted_iota(jnp.int32, (rows, lines), 0)
    line = lax.broadcasted_iota(jnp.int32, (rows, lines), 1)
    one = (lax.rem(row, slots) == slot_of) & (lax.div(row, slots) == lax.rem(line, steps))
    join = jnp.sum(jnp.where(one, step_of, 0.0), axis=1, keepdims=True).astype(jnp.int32)
    later = lax.broadcasted_iota(jnp.int32, (rows, rows), 0)
    earlier = lax.broadcasted_iota(jnp.int32, (rows, rows), 1)
    t_now, t_then = lax.div(later, slots), lax.div(earlier, slots)
    kept = (lax.rem(later, slots) == lax.rem(earlier, slots)) & (t_then <= t_now)
    kept = kept & ((t_then >= join) | (t_now < join))
    scores = lax.dot_general(q_ref[...], k_ref[...], (((1,), (1,)), ((), ())), preferred_element_type=F32)
    weights = jnp.where(kept, scores * int_power(decay, t_now - t_then, steps - 1), 0.0)
    coarse = weights.astype(BF16)
    fine = (weights - coarse.astype(F32)).astype(BF16)
    v = v_ref[...]
    carried = back[:, :width].astype(BF16)
    left = jnp.concatenate([jnp.where(one, 1.0, 0.0).astype(BF16), coarse, fine], axis=1)
    right = jnp.concatenate([carried, v, v], axis=0)
    readout = jnp.dot(left, right, preferred_element_type=F32)
    mean = jnp.sum(readout * readout, axis=1, keepdims=True) * (1.0 / width)
    normed = readout * lax.rsqrt(mean + 1e-06) * gain_ref[...] * g_ref[...].astype(F32)
    normed = normed.astype(BF16)
    shares, _, columns = out_ref.shape
    for share in range(0, shares, 2):
        part = jnp.dot(normed, w_ref[:, share * columns : (share + 2) * columns], preferred_element_type=F32)
        part = part.astype(out_ref.dtype)
        out_ref[HEAD_ORDER.index(share)] = part[:, 0:columns]
        out_ref[HEAD_ORDER.index(share + 1)] = part[:, columns:]


def total_kernel(shares_ref, out_ref):
    total = shares_ref[0].astype(F32)
    for share in range(1, shares_ref.shape[0]):
        total += shares_ref[share].astype(F32)
    out_ref[...] = total.astype(out_ref.dtype)


def call(kernel, name, out_shape, in_specs, out_specs, scratch=(), cost=None):
    return pl.pallas_call(
        kernel,
        out_shape=out_shape,
        in_specs=in_specs,
        out_specs=out_specs,
        scratch_shapes=scratch,
        compiler_params=pltpu.CompilerParams(vmem_limit_bytes=16 << 20),
        cost_estimate=cost,
        name=name,
    )


def shards(queries, keys, values, gates, prefill_states, dest_slot, arrive_step, decay, norm_gain, out_weight):
    steps, slots, key_dim = queries.shape
    val_dim = values.shape[2]
    rows = steps * slots
    per_source = dest_slot.shape[0]
    spacing = lax.axis_size("rows") // per_source
    sources, returns = [
        [[first + spacing * member for member in order] for first in range(spacing)]
        for order in (SOURCE_ORDER, RETURN_ORDER)
    ]
    shape = jax.ShapeDtypeStruct
    spread_size = per_source * rows * key_dim
    q = queries.reshape(rows, key_dim)
    states = prefill_states.reshape(per_source, key_dim, val_dim)
    spread, scale, pick, tail = call(
        lambda *refs: prepare_kernel(spacing, steps, slots, *refs),
        "spread_queries",
        (
            pltpu.VMEM((per_source, rows, key_dim), BF16),
            pltpu.VMEM((per_source, steps, 128), F32),
            pltpu.VMEM((per_source, slots, 128), F32),
            pltpu.VMEM((per_source, steps, TAIL), F32),
        ),
        [ANY, ANY, SMEM, ANY],
        (VMEM,) * 4,
        [
            pltpu.SMEM(dest_slot.shape, jnp.int32),
            pltpu.SMEM(arrive_step.shape, jnp.int32),
            pltpu.SemaphoreType.DMA((3,)),
        ],
        pl.CostEstimate(flops=20 * 10**9, bytes_accessed=2 * spread_size, transcendentals=0),
    )(in_hbm(dest_slot), in_hbm(arrive_step), decay, in_hbm(q))
    q_all = lax.all_to_all(spread, "rows", 0, 0, axis_index_groups=sources, tiled=True)
    readouts = call(
        lambda *refs: source_kernel(spacing, steps, slots, *refs),
        "source_readout",
        shape((per_source, steps, val_dim + TAIL), BF16),
        [VMEM] * 5,
        VMEM,
        cost=pl.CostEstimate(flops=20 * 10**9, bytes_accessed=2 * states.size, transcendentals=0),
    )(q_all, states, scale, pick, tail)
    back = lax.all_to_all(readouts, "rows", 0, 0, axis_index_groups=returns, tiled=True)
    heads = lax.axis_size("heads")
    columns = out_weight.shape[1] // heads
    partial = call(
        lambda *refs: row_kernel(steps, slots, *refs),
        "combine_project",
        shape((heads, rows, columns), BF16),
        [SMEM] + [VMEM] * 7,
        VMEM,
    )(
        decay, back, q, keys.reshape(rows, key_dim), values.reshape(rows, val_dim),
        gates.reshape(rows, val_dim), norm_gain.reshape(1, val_dim), out_weight,
    )
    shares = lax.all_to_all(partial, "heads", 0, 0, axis_index_groups=[list(HEAD_ORDER)], tiled=True)
    total = call(total_kernel, "sum_heads", shape((rows, columns), BF16), [VMEM], VMEM)(shares)
    return total.reshape(steps, slots, columns)


def solution(mesh):
    placed = (
        P(None, "rows", "heads"),
        P(None, "rows", "heads"),
        P(None, "rows", "heads"),
        P(None, "rows", "heads"),
        P("rows", "heads", None, None),
        P("rows"),
        P("rows"),
        P("heads"),
        P("heads"),
        P("heads", None),
    )
    return jax.shard_map(
        shards, mesh=mesh, in_specs=placed, out_specs=P(None, "rows", "heads"), check_vma=False
    )
```
